256 devices in a mesh: samp: 16 (over y_hi, z), par: 16 (over x, y_lo, core).
Axes of the slice: x: 4, y: 4 (y_hi: 2, y_lo: 2; y = y_hi * 2 + y_lo), z: 8, core: 2. Of those that a mesh axis runs over, the one named last changes fastest.
Arguments:
- log_derivs: bfloat16 [6144, 16384], P('samp', 'par'), may hold values from -30 to 30
Outputs:
- gram: float32 [6144, 6144], P(('samp', 'par'))
The draws below stay inside these ranges and needn't reach their ends.
All inputs are finite; a program needn't handle non-finite values.
Results may differ from the reference program's by a relative error of at most 0.00032.
Values may be sent and summed in bfloat16 or wider, within the bound.
No kernel may reach another device: no remote copies, remote signals or barrier semaphores. Data moves between devices by JAX's collectives and lax.ppermute only.
A program may use at most 64 MiB of HBM per device.

```python
import math
import jax
import jax.numpy as jnp
from jax import lax

PARAMS = 16384
SAMPLES = 6144


def draw_log_derivs(key, part):
    key = jax.random.fold_in(key, 11)
    keys = jax.random.split(key, 4)
    center = jnp.clip(jax.random.normal(keys[0], (PARAMS,), jnp.float32), -3.0, 3.0)
    row_scale = jnp.exp(jax.random.uniform(keys[1], (SAMPLES, 1), jnp.float32) * math.log(10.0))
    col_scale = jnp.exp(jax.random.uniform(keys[2], (1, PARAMS), jnp.float32) * math.log(10.0))
    noise = jnp.clip(jax.random.normal(keys[3], (SAMPLES, PARAMS), jnp.float32), -4.0, 4.0)
    ramp = 0.5 + 1.5 * jnp.arange(SAMPLES, dtype=jnp.float32)[:, None] / SAMPLES
    value = center[None, :] * ramp + 0.05 * row_scale * col_scale * noise
    return jnp.clip(value, -30.0, 30.0).astype(jnp.bfloat16)


def setup_inputs(seed: int = 0) -> dict:
    seeds = jax.random.split(jax.random.key(seed), 2)
    return {
        "log_derivs": draw_log_derivs(jax.random.fold_in(seeds[1], 71), 0),
    }


def reference(log_derivs):
    mean = lax.optimization_barrier(jnp.sum(log_derivs.astype(jnp.float32), axis=0)) / SAMPLES
    scale = 1.0 / jnp.sqrt(jnp.float32(SAMPLES))
    centered = ((log_derivs.astype(jnp.float32) - mean) * scale).astype(jnp.bfloat16)
    wide = centered.astype(jnp.float32)
    return jnp.dot(wide, wide.T, precision=lax.Precision.HIGHEST, preferred_element_type=jnp.float32)
```

```python
import jax
import jax.numpy as jnp
from jax import lax
from jax.sharding import Mesh, PartitionSpec as P

AXES = {"yh": 2, "z": 8, "x": 4, "yl": 2, "core": 2}
SAMP = ("yh", "z")
PAR = ("x", "yl", "core")

GROUPS = (
    (((0, 0), (0, 0)), ((0, 0), (0, 1)), ((0, 0), (0, -1)), ((0, -1), (0, 1)), ((0, 1), (0, -1))),
    (((0, 0), (1, 1)), ((0, 1), (1, 1)), ((0, -1), (1, 1)), ((1, 1), (0, 0)), ((1, 1), (0, -1))),
    (((0, -1), (0, 2)), ((0, 1), (0, -2)), ((0, -2), (0, 2)), ((0, -2), (1, 1)), ((1, 1), (0, -2))),
    (((0, -2), (1, 2)),),
)


def send(value, offset):
    ny, nz = AXES["yh"], AXES["z"]
    dy, dz = offset
    pairs = [
        (y * nz + z, (y + dy) % ny * nz + (z + dz) % nz) for y in range(ny) for z in range(nz)
    ]
    return lax.ppermute(value, SAMP, pairs)


def fetch(value, offset):
    return send(value, (-offset[0], -offset[1]))


def shift(value, axis, step):
    n = AXES[axis]
    return lax.ppermute(value, axis, [(i, (i + step) % n) for i in range(n)])


def column_sums(block):
    total = jnp.sum(block.astype(jnp.float32), axis=0).reshape(-1, 128)
    for offsets in (((0, 2), (0, 4), (0, 6)), ((0, 1), (1, 0), (1, 1))):
        parts = [fetch(total, offset) for offset in offsets]
        total = total + parts[0] + parts[1] + parts[2]
    return total.reshape(-1)


def reduce_over_par(value):
    rows, cols = value.shape
    value = value.reshape(2, rows // 2, cols)
    value = value[0] + shift(value[1], "core", 1)
    value = value.reshape(4, rows // 8, cols)
    parts = [shift(value[step], "x", step) for step in (1, 2, 3)]
    value = value[0] + parts[0] + parts[1] + parts[2]
    value = value.reshape(2, rows // 16, cols)
    return value[0] + shift(value[1], "yl", 1)


def local(block):
    rows = block.shape[0]
    half, chunk = rows // 2, rows // 16
    blocks = AXES["yh"] * AXES["z"]
    total_rows = rows * blocks

    halves = {(0, 0): [block[:half], block[half:]]}
    halves[0, 1] = [fetch(h, (0, 1)) for h in halves[0, 0]]
    halves[0, -1] = [fetch(h, (0, -1)) for h in halves[0, 0]]
    halves[1, 1] = [fetch(h, (1, 0)) for h in halves[0, 1]]
    halves[0, 2] = [fetch(h, (0, 1)) for h in halves[0, 1]]
    halves[0, -2] = [fetch(h, (0, -1)) for h in halves[0, -1]]
    halves[1, 2] = [fetch(h, (1, 0)) for h in halves[0, 2]]

    mean = column_sums(block) / total_rows
    scale = 1.0 / jnp.sqrt(jnp.float32(total_rows))

    def centre(part):
        return ((part.astype(jnp.float32) - mean) * scale).astype(jnp.bfloat16)

    centred = {
        offset: jnp.concatenate([centre(h) for h in parts], axis=0)
        for offset, parts in halves.items()
    }

    ix, iy, ic, sy, sz = (
        lax.axis_index(axis).astype(jnp.uint32) for axis in ("x", "yl", "core", "yh", "z")
    )
    order = [
        ((ix + rx) & 3) * 4 + ((iy + ry) & 1) * 2 + ((ic + rc) & 1)
        for rc in range(2)
        for rx in range(4)
        for ry in range(2)
    ]

    def relative(value):
        parts = value.reshape(16, chunk, -1)
        return jnp.concatenate(
            [lax.dynamic_index_in_dim(parts, i, 0, keepdims=False) for i in order], axis=0
        )

    lefts = {}
    for group in GROUPS:
        for left, _ in group:
            if left not in lefts:
                lefts[left] = relative(centred[left])

    out = jnp.zeros((chunk, total_rows), jnp.float32)
    for group in GROUPS:
        products = [
            lax.dot_general(
                lefts[left],
                centred[right],
                (((1,), (1,)), ((), ())),
                preferred_element_type=jnp.float32,
            )
            for left, right in group
        ]
        done = reduce_over_par(jnp.concatenate(products, axis=1))
        for lead in dict.fromkeys(left for left, _ in group):
            members = [n for n, (left, _) in enumerate(group) if left == lead]
            piece = jnp.concatenate([done[:, n * rows : (n + 1) * rows] for n in members], axis=1)
            if lead != (0, 0):
                piece = send(piece, lead)
            for k, n in enumerate(members):
                left, right = group[n]
                dy, dz = right[0] - left[0], right[1] - left[1]
                place = ((sy + (dy & 1)) & 1) * 8 + ((sz + (dz & 7)) & 7)
                out = lax.dynamic_update_slice(
                    out, piece[:, k * rows : (k + 1) * rows], (jnp.uint32(0), place * rows)
                )
    return out


def solution(mesh):
    fine = Mesh(mesh.devices.reshape(tuple(AXES.values())), tuple(AXES))
    return jax.shard_map(
        local,
        mesh=fine,
        in_specs=(P(SAMP, PAR),),
        out_specs=P(SAMP + PAR, None),
        check_vma=False,
    )
```

```python
import jax
import jax.numpy as jnp
from jax import lax
from jax.sharding import Mesh, PartitionSpec as P

AXES = {"yh": 2, "z": 8, "x": 4, "yl": 2, "core": 2}
SAMP = ("yh", "z")
PAR = ("x", "yl", "core")

SLOTS = {
    "S0": ((0, 0), (0, 0)),
    "S1": ((0, 1), (0, -1)),
    "S2": ((0, 2), (0, -2)),
    "T1": ((0, 0), (1, 0)),
    "T2": ((0, -1), (1, 1)),
    "T3": ((0, -2), (1, 2)),
}
GROUPS = (
    (("S0", "T1"), ("T1", "S1")),
    (("S0", "T2"), ("T1", "S2"), ("S2", "T2"), ("T2", "S2")),
    (("S0", "T3"), ("S2", "T3")),
)


def permute(value, route):
    sizes = tuple(AXES.values())

    def number(place):
        index = 0
        for coordinate, size in zip(place, sizes):
            index = index * size + coordinate % size
        return index

    places = [
        (y, z, x, l, c)
        for y in range(sizes[0])
        for z in range(sizes[1])
        for x in range(sizes[2])
        for l in range(sizes[3])
        for c in range(sizes[4])
    ]
    pairs = [(number(p), number(route(*p))) for p in places if route(*p) is not None]
    return lax.ppermute(value, tuple(AXES), pairs)


def along_z(y, z, x, l, c):
    return (y, z - 1 if c == 0 else z + 1, x, l, c)


def along_z_other(y, z, x, l, c):
    return (y, z + 1, x, l, 1) if c == 0 else (y, z - 1, x, l, 0)


def across_y(y, z, x, l, c):
    return (y + 1, z, x, l, 1) if c == 1 else None


def across_y_other(y, z, x, l, c):
    return (y + 1, z, x, l, 1) if c == 0 else None


def crossing(y, z, x, l, c):
    return (y + 1, z, x, l, 1) if c == 0 else (y, z, x, l, 0)


def other_core(y, z, x, l, c):
    return (y, z, x, l, 1 - c)


def to_offset(dy, dz):
    return lambda y, z, x, l, c: (y + dy, z + dz, x, l, c)


def scatter_over_par(value):
    rows, cols = value.shape
    exponent = jnp.clip(jnp.ceil(jnp.log2(jnp.max(jnp.abs(value)))), -100.0, 20.0)
    scaled = (value * jnp.exp2(14.0 - exponent)).astype(jnp.float16)
    note = jnp.full((rows, 128), exponent, jnp.float32).astype(jnp.float16)
    message = jnp.concatenate([scaled, note], axis=1).reshape(16, rows // 16, cols + 128)
    return lax.all_to_all(message, PAR, 0, 0)


def gather_sum(message):
    _, chunk, width = message.shape
    cols = width - 128
    factor = jnp.exp2(message[:, :1, cols : cols + 1].astype(jnp.float32) - 14.0)
    parts = message[:, :, :cols].astype(jnp.float32) * factor
    return jnp.sum(parts.reshape(8, 2, chunk, cols), axis=0)


def local(block):
    rows = block.shape[0]
    chunk = rows // 16
    blocks = AXES["yh"] * AXES["z"]
    total_rows = rows * blocks
    sy, sz, core = (lax.axis_index(axis).astype(jnp.uint32) for axis in ("yh", "z", "core"))
    in_order = lax.optimization_barrier

    other = permute(block, other_core)
    near = permute(block, along_z), permute(block, along_z_other)
    mate = permute(block, across_y), permute(block, across_y_other)

    sums = jnp.concatenate(
        [jnp.sum(part.astype(jnp.float32), axis=0) for part in (block, other)]
    ).reshape(-1, 128)
    sums = lax.all_to_all(jnp.broadcast_to(sums, (blocks, *sums.shape)), SAMP, 0, 0)
    mean = jnp.sum(sums, axis=0).reshape(2, 1, -1) / total_rows
    scale = 1.0 / jnp.sqrt(jnp.float32(total_rows))

    def centre(own, others):
        return jnp.concatenate(
            [
                ((part.astype(jnp.float32) - mean[n]) * scale).astype(jnp.bfloat16)
                for n, part in enumerate((own, others))
            ],
            axis=1,
        )

    def scatter(group):
        products = [
            lax.dot_general(
                held[left],
                held[right],
                (((1,), (1,)), ((), ())),
                preferred_element_type=jnp.float32,
            )
            for left, right in group
        ]
        return scatter_over_par(jnp.concatenate(products, axis=1))

    held = {"S0": in_order(centre(block, other))}
    mean, near, mate = in_order((mean, near, mate))
    near = jnp.concatenate(near, axis=0)
    far = permute(near, along_z)
    near_crossed = permute(near, crossing)
    held["S1"] = centre(near[:rows], near[rows:])
    held["T1"] = in_order(jnp.where(core == 1, centre(*mate), held["S0"]))
    messages = [scatter(GROUPS[0])]

    messages[0], far, near_crossed = in_order((messages[0], far, near_crossed))
    far_crossed = permute(far, crossing)
    held["S2"] = centre(far[:rows], far[rows:])
    held["T2"] = centre(near_crossed[rows:], near_crossed[:rows])
    messages.append(scatter(GROUPS[1]))

    messages[1], far_crossed = in_order((messages[1], far_crossed))
    held["T3"] = centre(far_crossed[rows:], far_crossed[:rows])
    messages.append(scatter(GROUPS[2]))

    finished = {}
    for group, message in zip(GROUPS, messages):
        done = gather_sum(message)
        for n, (left, right) in enumerate(group):
            for c in range(2):
                a, b = SLOTS[left][c], SLOTS[right][c]
                offset = (b[0] - a[0]) % 2, (b[1] - a[1]) % 8
                finished.setdefault((a[0] % 2, a[1] % 8), []).append(
                    (offset, done[c, :, n * rows : (n + 1) * rows])
                )

    out = jnp.zeros((chunk, total_rows), jnp.float32)
    for lead, items in finished.items():
        piece = [value for _, value in items]
        if lead != (0, 0):
            moved = permute(jnp.concatenate(piece, axis=1), to_offset(*lead))
            piece = [moved[:, k * rows : (k + 1) * rows] for k in range(len(items))]
        for (offset, _), value in zip(items, piece):
            place = ((sy + offset[0]) & 1) * 8 + ((sz + offset[1]) & 7)
            out = lax.dynamic_update_slice(out, value, (jnp.uint32(0), place * rows))
    return out


def solution(mesh):
    fine = Mesh(mesh.devices.reshape(tuple(AXES.values())), tuple(AXES))
    return jax.shard_map(
        local,
        mesh=fine,
        in_specs=(P(SAMP, PAR),),
        out_specs=P(SAMP + PAR, None),
        check_vma=False,
    )
```

```python
import functools

import jax
import jax.numpy as jnp
import numpy as np
from jax import lax
from jax.experimental import pallas as pl
from jax.experimental.pallas import tpu as pltpu
from jax.sharding import Mesh, PartitionSpec as P

AXES = {"yh": 2, "z": 8, "x": 4, "yl": 2, "core": 2}
SAMP = ("yh", "z")
PAR = ("x", "yl", "core")
VMEM_MIB = 16

SLOTS = {
    "S0": ((0, 0), (0, 0)),
    "S1": ((0, 1), (0, -1)),
    "S2": ((0, 2), (0, -2)),
    "T1": ((0, 0), (1, 0)),
    "T3": ((0, -2), (1, 2)),
}
GROUPS = (
    ((("S0", "T1"),) * 2, (("S1", "T1"),) * 2, (("T1", "S1"),) * 2),
    ((("S0", "T3"),) * 2, (("T3", "S0"),) * 2, (("S1", "T3"),) * 2, (("T3", "S1"),) * 2),
    ((("T3", "S2"), ("S2", "T3")),),
)


def permute(value, route):
    sizes = tuple(AXES.values())

    def number(place):
        index = 0
        for coordinate, size in zip(place, sizes):
            index = index * size + coordinate % size
        return index

    places = [
        (y, z, x, l, c)
        for y in range(sizes[0])
        for z in range(sizes[1])
        for x in range(sizes[2])
        for l in range(sizes[3])
        for c in range(sizes[4])
    ]
    pairs = [(number(p), number(route(*p))) for p in places if route(*p) is not None]
    return lax.ppermute(value, tuple(AXES), pairs)


def along_z(y, z, x, l, c):
    return (y, z - 1 if c == 0 else z + 1, x, l, c)


def across_y(y, z, x, l, c):
    return (y + 1, z, x, l, 1) if c == 1 else None


def crossing(y, z, x, l, c):
    return (y + 1, z - 1, x, l, 1) if c == 0 else (y, z + 1, x, l, 0)


def other_core(y, z, x, l, c):
    return (y, z, x, l, 1 - c)


def to_offset(dy, dz):
    return lambda y, z, x, l, c: (y + dy, z + dz, x, l, c)


def multiply_kernel(raw, held, kept, group, scale, core_ref, mean_ref, *refs):
    raw_refs, refs = refs[: len(raw)], refs[len(raw) :]
    held_refs, kept_refs, out_ref = refs[: len(held)], refs[len(held) : -1], refs[-1]
    rows, width = raw_refs[0].shape[0] // 2, raw_refs[0].shape[1]
    cols = out_ref.shape[1] - 128
    on_core_1 = core_ref[0] == 1

    terms = [[] for _ in group]
    for half in range(2):
        across = slice(half * width, (half + 1) * width)
        mean = mean_ref[0:1, across]
        wide = {}
        for ref, (name, flip) in zip(raw_refs, raw):
            first = (1 - half if flip else half) * rows
            wide[name] = ref[first : first + rows, :].astype(jnp.float32)
        if "T1" in wide:
            wide["T1"] = jnp.where(on_core_1, wide["T1"], wide["S0"])
        blocks = {
            name: ((value - mean) * scale).astype(jnp.bfloat16) for name, value in wide.items()
        }
        for ref, name in zip(kept_refs, kept):
            ref[:, across] = blocks[name]
        for ref, name in zip(held_refs, held):
            blocks[name] = ref[:, across]
        for term, ((left, right), (left_1, right_1)) in zip(terms, group):
            left, right = blocks[left], blocks[right]
            if left_1 != left:
                left = jnp.where(on_core_1, blocks[left_1], left)
                right = jnp.where(on_core_1, blocks[right_1], right)
            term.append(
                lax.dot_general(
                    left, right, (((1,), (1,)), ((), ())), preferred_element_type=jnp.float32
                )
            )
    largest = jnp.zeros((1, 1), jnp.float32)
    for n, (first, second) in enumerate(terms):
        total = first + second
        out_ref[:, n * rows : (n + 1) * rows] = total
        largest = jnp.maximum(largest, jnp.max(jnp.abs(total), keepdims=True))
    exponent = jnp.clip(jnp.ceil(jnp.log2(largest)), -100.0, 20.0)
    out_ref[:, :cols] *= jnp.exp2(14.0 - exponent)
    out_ref[:, cols:] = jnp.broadcast_to(exponent, (rows, 128))


def multiply(core, mean, raw, held, kept, group, scale):
    first = next(iter(raw.values()))[0]
    rows, width = first.shape[0] // 2, 2 * first.shape[1]
    cols = len(group) * rows
    whole = pl.BlockSpec(memory_space=pltpu.VMEM)
    centred = jax.ShapeDtypeStruct((rows, width), jnp.bfloat16)
    names = tuple((name, flip) for name, (_, flip) in raw.items())
    *blocks, value = pl.pallas_call(
        functools.partial(multiply_kernel, names, tuple(held), kept, group, scale),
        in_specs=[pl.BlockSpec(memory_space=pltpu.SMEM)] + [whole] * (1 + len(raw) + len(held)),
        out_specs=[whole] * (len(kept) + 1),
        out_shape=[*(centred for _ in kept), jax.ShapeDtypeStruct((rows, cols + 128), jnp.float32)],
        compiler_params=pltpu.CompilerParams(vmem_limit_bytes=VMEM_MIB * 2**20),
        cost_estimate=pl.CostEstimate(flops=1, bytes_accessed=1, transcendentals=0),
    )(core, mean, *(block for block, _ in raw.values()), *held.values())
    return dict(zip(kept, blocks)), value


def scatter_over_par(value):
    rows, width = value.shape
    message = value.astype(jnp.float16).reshape(16, rows // 16, width)
    return lax.all_to_all(message, PAR, 0, 0)


def gather_sum(message):
    _, chunk, width = message.shape
    message = message.reshape(8, 2, chunk, width)
    factor = jnp.exp2(message[:, :, :1, width - 128 : width - 127].astype(jnp.float32) - 14.0)
    return jnp.sum(message[:, :, :, : width - 128].astype(jnp.float32) * factor, axis=0)


def place_kernel(pieces, place_ref, *refs):
    out_ref = refs[-1]
    for n, (source, index) in enumerate(pieces):
        value = refs[source][index]
        width = value.shape[1]
        out_ref[:, pl.ds(pl.multiple_of(place_ref[n] * width, 128), width)] = value


def local(block):
    rows = block.shape[0]
    chunk = rows // 16
    blocks = AXES["yh"] * AXES["z"]
    total_rows = rows * blocks
    sy, sz, core = (lax.axis_index(axis).astype(jnp.int32) for axis in ("yh", "z", "core"))
    core = core.reshape(1)

    own = jnp.concatenate([block, permute(block, other_core)], axis=0)
    near = permute(own, along_z)
    mate = permute(own, across_y)

    sums = [jnp.sum(part.astype(jnp.float32), axis=0) for part in (own[:rows], own[rows:])]
    sums = jnp.concatenate(sums).reshape(-1, 128)
    sums = lax.all_to_all(jnp.broadcast_to(sums, (blocks, *sums.shape)), SAMP, 0, 0)
    near, mate, sums = lax.optimization_barrier((near, mate, sums))
    crossed = permute(near, crossing)
    mean = jnp.sum(sums, axis=0).reshape(1, -1) / total_rows
    mean = jnp.broadcast_to(mean, (8, mean.shape[1]))
    scale = float(np.float32(1) / np.sqrt(np.float32(total_rows)))

    raw = {"S0": (own, False), "S1": (near, False), "T1": (mate, False)}
    held, value = multiply(core, mean, raw, {}, ("S0", "S1"), GROUPS[0], scale)
    messages = [scatter_over_par(value)]
    held, value = multiply(core, mean, {"T3": (crossed, True)}, held, ("T3",), GROUPS[1], scale)
    near, value = lax.optimization_barrier((near, value))
    far = permute(near, along_z)
    messages.append(scatter_over_par(value))
    _, value = multiply(core, mean, {"S2": (far, False)}, held, (), GROUPS[2], scale)
    messages[1], value = lax.optimization_barrier((messages[1], value))
    messages.append(scatter_over_par(value))

    sources, pieces, places = [], [], []

    def move(leads):
        for lead, items in leads.items():
            value = jnp.concatenate([value for _, value in items], axis=1)
            moved.append(permute(value, to_offset(*lead)))
            for n, (offset, _) in enumerate(items):
                across = slice(n * rows, (n + 1) * rows)
                pieces.append((len(sources) + len(moved) - 1, (slice(None), across)))
                places.append(offset)

    leads = {}
    for n, (group, message) in enumerate(zip(GROUPS, messages)):
        moved = []
        if n == len(GROUPS) - 1:
            move(leads)
            leads = {}
            *moved, message = lax.optimization_barrier((*moved, message))
            sources += moved
            moved = []
        done = gather_sum(message)
        sources.append(done)
        for k, pairs in enumerate(group):
            across = slice(k * rows, (k + 1) * rows)
            for c, (left, right) in enumerate(pairs):
                a, b = SLOTS[left][c], SLOTS[right][c]
                offset = (b[0] - a[0]) & 1, (b[1] - a[1]) & 7
                lead = a[0] & 1, a[1] & 7
                if lead == (0, 0):
                    pieces.append((len(sources) - 1, (c, slice(None), across)))
                    places.append(offset)
                else:
                    leads.setdefault(lead, []).append((offset, done[c, :, across]))
    move(leads)
    sources += moved
    place = jnp.stack([((sy + dy) & 1) * 8 + ((sz + dz) & 7) for dy, dz in places])
    whole = pl.BlockSpec(memory_space=pltpu.VMEM)
    return pl.pallas_call(
        functools.partial(place_kernel, tuple(pieces)),
        in_specs=[pl.BlockSpec(memory_space=pltpu.SMEM), *(whole for _ in sources)],
        out_specs=whole,
        out_shape=jax.ShapeDtypeStruct((chunk, total_rows), jnp.float32),
        compiler_params=pltpu.CompilerParams(vmem_limit_bytes=8 * 2**20),
    )(place, *sources)


def solution(mesh):
    fine = Mesh(mesh.devices.reshape(tuple(AXES.values())), tuple(AXES))
    return jax.shard_map(
        local,
        mesh=fine,
        in_specs=(P(SAMP, PAR),),
        out_specs=P(SAMP + PAR, None),
        check_vma=False,
    )
```

```python
import functools

import jax
import jax.numpy as jnp
import numpy as np
from jax import lax
from jax.experimental import pallas as pl
from jax.experimental.pallas import tpu as pltpu
from jax.sharding import Mesh, PartitionSpec as P

AXES = {"yh": 2, "z": 8, "x": 4, "yl": 2, "core": 2}
SAMP = ("yh", "z")
PAR = ("x", "yl", "core")
VMEM_MIB = 16

SLOTS = {
    "S0": ((0, 0), (0, 0)),
    "S1": ((0, 1), (0, -1)),
    "S2": ((0, 2), (0, -2)),
    "T1": ((0, 0), (1, 0)),
    "T3": ((0, -2), (1, 2)),
}
GROUPS = (
    ((("S0", "T1"),) * 2, (("S1", "T1"),) * 2, (("T1", "S1"),) * 2),
    ((("T3", "S0"),) * 2, (("S1", "T3"),) * 2, (("T3", "S1"),) * 2),
    ((("S0", "T3"),) * 2, (("T3", "S2"), ("S2", "T3"))),
)


def permute(value, route):
    sizes = tuple(AXES.values())

    def number(place):
        index = 0
        for coordinate, size in zip(place, sizes):
            index = index * size + coordinate % size
        return index

    places = [
        (y, z, x, l, c)
        for y in range(sizes[0])
        for z in range(sizes[1])
        for x in range(sizes[2])
        for l in range(sizes[3])
        for c in range(sizes[4])
    ]
    pairs = [(number(p), number(route(*p))) for p in places if route(*p) is not None]
    return lax.ppermute(value, tuple(AXES), pairs)


def along_z(y, z, x, l, c):
    return (y, z - 1 if c == 0 else z + 1, x, l, c)


def across_y(y, z, x, l, c):
    return (y + 1, z, x, l, 1) if c == 1 else None


def crossing(y, z, x, l, c):
    return (y + 1, z - 1, x, l, 1) if c == 0 else (y, z + 1, x, l, 0)


def other_core(y, z, x, l, c):
    return (y, z, x, l, 1 - c)


def to_offset(dy, dz):
    return lambda y, z, x, l, c: (y + dy, z + dz, x, l, c)


def multiply_kernel(raw, held, kept, group, scale, core_ref, mean_ref, *refs):
    raw_refs, refs = refs[: len(raw)], refs[len(raw) :]
    held_refs, kept_refs, out_ref = refs[: len(held)], refs[len(held) : -1], refs[-1]
    rows, width = raw_refs[0].shape[0] // 2, raw_refs[0].shape[1]
    cols = out_ref.shape[1] - 128
    on_core_1 = core_ref[0] == 1

    terms = [[] for _ in group]
    for half in range(2):
        across = slice(half * width, (half + 1) * width)
        mean = mean_ref[0:1, across]
        wide = {}
        for ref, (name, flip) in zip(raw_refs, raw):
            first = (1 - half if flip else half) * rows
            wide[name] = ref[first : first + rows, :].astype(jnp.float32)
        if "T1" in wide:
            wide["T1"] = jnp.where(on_core_1, wide["T1"], wide["S0"])
        blocks = {
            name: ((value - mean) * scale).astype(jnp.bfloat16) for name, value in wide.items()
        }
        for ref, name in zip(kept_refs, kept):
            ref[:, across] = blocks[name]
        for ref, name in zip(held_refs, held):
            blocks[name] = ref[:, across]
        for term, ((left, right), (left_1, right_1)) in zip(terms, group):
            left, right = blocks[left], blocks[right]
            if left_1 != left:
                left = jnp.where(on_core_1, blocks[left_1], left)
                right = jnp.where(on_core_1, blocks[right_1], right)
            term.append(
                lax.dot_general(
                    left, right, (((1,), (1,)), ((), ())), preferred_element_type=jnp.float32
                )
            )
    largest = jnp.zeros((1, 1), jnp.float32)
    for n, (first, second) in enumerate(terms):
        total = first + second
        out_ref[:, n * rows : (n + 1) * rows] = total
        largest = jnp.maximum(largest, jnp.max(jnp.abs(total), keepdims=True))
    exponent = jnp.clip(jnp.ceil(jnp.log2(largest)), -100.0, 20.0)
    out_ref[:, :cols] *= jnp.exp2(14.0 - exponent)
    out_ref[:, cols:] = jnp.broadcast_to(exponent, (rows, 128))


def multiply(core, mean, raw, held, kept, group, scale):
    first = next(iter(raw.values()))[0]
    rows, width = first.shape[0] // 2, 2 * first.shape[1]
    cols = len(group) * rows
    whole = pl.BlockSpec(memory_space=pltpu.VMEM)
    centred = jax.ShapeDtypeStruct((rows, width), jnp.bfloat16)
    names = tuple((name, flip) for name, (_, flip) in raw.items())
    *blocks, value = pl.pallas_call(
        functools.partial(multiply_kernel, names, tuple(held), kept, group, scale),
        in_specs=[pl.BlockSpec(memory_space=pltpu.SMEM)] + [whole] * (1 + len(raw) + len(held)),
        out_specs=[whole] * (len(kept) + 1),
        out_shape=[*(centred for _ in kept), jax.ShapeDtypeStruct((rows, cols + 128), jnp.float32)],
        compiler_params=pltpu.CompilerParams(vmem_limit_bytes=VMEM_MIB * 2**20),
        cost_estimate=pl.CostEstimate(flops=1, bytes_accessed=1, transcendentals=0),
    )(core, mean, *(block for block, _ in raw.values()), *held.values())
    return dict(zip(kept, blocks)), value


def message_of(value):
    rows, width = value.shape
    return value.astype(jnp.float16).reshape(16, rows // 16, width)


def scatter_over_par(message):
    return lax.all_to_all(message, PAR, 0, 0)


def gather_sum(message):
    _, chunk, width = message.shape
    message = message.reshape(8, 2, chunk, width)
    factor = jnp.exp2(message[:, :, :1, width - 128 : width - 127].astype(jnp.float32) - 14.0)
    return jnp.sum(message[:, :, :, : width - 128].astype(jnp.float32) * factor, axis=0)


def place_kernel(pieces, place_ref, *refs):
    out_ref = refs[-1]
    for n, (source, index) in enumerate(pieces):
        value = refs[source][index]
        width = value.shape[1]
        out_ref[:, pl.ds(pl.multiple_of(place_ref[n] * width, 128), width)] = value


def local(block):
    rows = block.shape[0]
    chunk = rows // 16
    blocks = AXES["yh"] * AXES["z"]
    total_rows = rows * blocks
    sy, sz, core = (lax.axis_index(axis).astype(jnp.int32) for axis in ("yh", "z", "core"))
    core = core.reshape(1)

    own = jnp.concatenate([block, permute(block, other_core)], axis=0)
    near = permute(own, along_z)
    mate = permute(own, across_y)

    sums = [jnp.sum(part.astype(jnp.float32), axis=0) for part in (own[:rows], own[rows:])]
    sums = jnp.concatenate(sums).reshape(-1, 128)
    sums = lax.all_to_all(jnp.broadcast_to(sums, (blocks, *sums.shape)), SAMP, 0, 0)
    near, mate, sums = lax.optimization_barrier((near, mate, sums))
    crossed = permute(near, crossing)
    mean = jnp.sum(sums, axis=0).reshape(1, -1) / total_rows
    mean = jnp.broadcast_to(mean, (8, mean.shape[1]))
    scale = float(np.float32(1) / np.sqrt(np.float32(total_rows)))

    raw = {"S0": (own, False), "S1": (near, False), "T1": (mate, False)}
    held, value = multiply(core, mean, raw, {}, ("S0", "S1"), GROUPS[0], scale)
    messages = [scatter_over_par(message_of(value))]
    near, held["S1"] = lax.optimization_barrier((near, held["S1"]))
    far = permute(near, along_z)
    _, value = multiply(core, mean, {"T3": (crossed, True)}, held, (), GROUPS[1], scale)
    messages.append(scatter_over_par(message_of(value)))
    far, crossed, _ = lax.optimization_barrier((far, crossed, value))
    raw = {"S2": (far, False), "T3": (crossed, True)}
    _, value = multiply(core, mean, raw, {"S0": held["S0"]}, (), GROUPS[2], scale)
    messages[1], message = lax.optimization_barrier((messages[1], message_of(value)))
    messages.append(scatter_over_par(message))

    sources, pieces, places = [], [], []
    for group, message in zip(GROUPS, messages):
        *sources, message = lax.optimization_barrier((*sources, message))
        done = gather_sum(message)
        sources.append(done)
        leads = {}
        for k, pairs in enumerate(group):
            across = slice(k * rows, (k + 1) * rows)
            for c, (left, right) in enumerate(pairs):
                a, b = SLOTS[left][c], SLOTS[right][c]
                offset = (b[0] - a[0]) & 1, (b[1] - a[1]) & 7
                lead = a[0] & 1, a[1] & 7
                if lead == (0, 0):
                    pieces.append((len(sources) - 1, (c, slice(None), across)))
                    places.append(offset)
                else:
                    leads.setdefault(lead, []).append((offset, done[c, :, across]))
        for lead, items in leads.items():
            value = jnp.concatenate([value for _, value in items], axis=1)
            sources.append(permute(value, to_offset(*lead)))
            for n, (offset, _) in enumerate(items):
                across = slice(n * rows, (n + 1) * rows)
                pieces.append((len(sources) - 1, (slice(None), across)))
                places.append(offset)
    place = jnp.stack([((sy + dy) & 1) * 8 + ((sz + dz) & 7) for dy, dz in places])
    whole = pl.BlockSpec(memory_space=pltpu.VMEM)
    return pl.pallas_call(
        functools.partial(place_kernel, tuple(pieces)),
        in_specs=[pl.BlockSpec(memory_space=pltpu.SMEM), *(whole for _ in sources)],
        out_specs=whole,
        out_shape=jax.ShapeDtypeStruct((chunk, total_rows), jnp.float32),
        compiler_params=pltpu.CompilerParams(vmem_limit_bytes=8 * 2**20),
    )(place, *sources)


def solution(mesh):
    fine = Mesh(mesh.devices.reshape(tuple(AXES.values())), tuple(AXES))
    return jax.shard_map(
        local,
        mesh=fine,
        in_specs=(P(SAMP, PAR),),
        out_specs=P(SAMP + PAR, None),
        check_vma=False,
    )
```

```python
import functools

import jax
import jax.numpy as jnp
import numpy as np
from jax import lax
from jax.experimental import pallas as pl
from jax.experimental.pallas import tpu as pltpu
from jax.sharding import Mesh, PartitionSpec as P

AXES = {"yh": 2, "z": 8, "x": 4, "yl": 2, "core": 2}
SAMP = ("yh", "z")
PAR = ("x", "yl", "core")
VMEM_MIB = 16

SLOTS = {
    "S0": ((0, 0), (0, 0)),
    "S1": ((0, 1), (0, -1)),
    "S2": ((0, 2), (0, -2)),
    "T1": ((0, 0), (1, 0)),
    "T3": ((0, -2), (1, 2)),
}
GROUPS = (
    ((("S0", "T1"),) * 2, (("S1", "T1"),) * 2, (("T1", "S1"),) * 2),
    ((("T3", "S0"),) * 2, (("S1", "T3"),) * 2, (("T3", "S1"),) * 2),
    ((("S0", "T3"),) * 2, (("T3", "S2"), ("S2", "T3"))),
)


def permute(value, route):
    sizes = tuple(AXES.values())

    def number(place):
        index = 0
        for coordinate, size in zip(place, sizes):
            index = index * size + coordinate % size
        return index

    places = [
        (y, z, x, l, c)
        for y in range(sizes[0])
        for z in range(sizes[1])
        for x in range(sizes[2])
        for l in range(sizes[3])
        for c in range(sizes[4])
    ]
    pairs = [(number(p), number(route(*p))) for p in places if route(*p) is not None]
    return lax.ppermute(value, tuple(AXES), pairs)


def along_z(y, z, x, l, c):
    return (y, z - 1 if c == 0 else z + 1, x, l, c)


def across_y(y, z, x, l, c):
    return (y + 1, z, x, l, 1) if c == 1 else None


def crossing(y, z, x, l, c):
    return (y + 1, z - 1, x, l, 1) if c == 0 else (y, z + 1, x, l, 0)


def other_core(y, z, x, l, c):
    return (y, z, x, l, 1 - c)


def to_offset(dy, dz):
    return lambda y, z, x, l, c: (y + dy, z + dz, x, l, c)


def multiply_kernel(raw, held, kept, group, scale, core_ref, mean_ref, *refs):
    raw_refs, refs = refs[: len(raw)], refs[len(raw) :]
    held_refs, kept_refs, out_ref = refs[: len(held)], refs[len(held) : -1], refs[-1]
    rows, width = raw_refs[0].shape[0] // 2, raw_refs[0].shape[1]
    on_core_1 = core_ref[0] == 1

    terms = [[] for _ in group]
    for half in range(2):
        across = slice(half * width, (half + 1) * width)
        mean = mean_ref[0:1, across]
        wide = {}
        for ref, (name, flip) in zip(raw_refs, raw):
            first = (1 - half if flip else half) * rows
            wide[name] = ref[first : first + rows, :].astype(jnp.float32)
        if "T1" in wide:
            wide["T1"] = jnp.where(on_core_1, wide["T1"], wide["S0"])
        blocks = {
            name: ((value - mean) * scale).astype(jnp.bfloat16) for name, value in wide.items()
        }
        for ref, name in zip(kept_refs, kept):
            ref[:, across] = blocks[name]
        for ref, name in zip(held_refs, held):
            blocks[name] = ref[:, across]
        for term, ((left, right), (left_1, right_1)) in zip(terms, group):
            left, right = blocks[left], blocks[right]
            if left_1 != left:
                left = jnp.where(on_core_1, blocks[left_1], left)
                right = jnp.where(on_core_1, blocks[right_1], right)
            term.append(
                lax.dot_general(
                    left, right, (((1,), (1,)), ((), ())), preferred_element_type=jnp.float32
                )
            )
    totals = [first + second for first, second in terms]
    largest = jnp.zeros((1, 1), jnp.float32)
    for total in totals:
        largest = jnp.maximum(largest, jnp.max(jnp.abs(total), keepdims=True))
    exponent = jnp.clip(jnp.ceil(jnp.log2(largest)), -100.0, 20.0)
    factor = jnp.exp2(14.0 - exponent)
    tile = 0
    for total in totals:
        scaled = (total * factor).reshape(16, rows // 128, 8, rows)
        for deep in range(rows // 128):
            for begin in range(0, rows, 128):
                out_ref[:, tile] = scaled[:, deep, :, begin : begin + 128]
                tile += 1
    out_ref[:, tile] = jnp.broadcast_to(exponent.reshape(1, 1, 1), (16, 8, 128))


def multiply(core, mean, raw, held, kept, group, scale):
    first = next(iter(raw.values()))[0]
    rows, width = first.shape[0] // 2, 2 * first.shape[1]
    tiles = len(group) * (rows // 128) ** 2 + 1
    whole = pl.BlockSpec(memory_space=pltpu.VMEM)
    centred = jax.ShapeDtypeStruct((rows, width), jnp.bfloat16)
    names = tuple((name, flip) for name, (_, flip) in raw.items())
    *blocks, value = pl.pallas_call(
        functools.partial(multiply_kernel, names, tuple(held), kept, group, scale),
        in_specs=[pl.BlockSpec(memory_space=pltpu.SMEM)] + [whole] * (1 + len(raw) + len(held)),
        out_specs=[whole] * (len(kept) + 1),
        out_shape=[*(centred for _ in kept), jax.ShapeDtypeStruct((16, tiles, 8, 128), jnp.float32)],
        compiler_params=pltpu.CompilerParams(vmem_limit_bytes=VMEM_MIB * 2**20),
        cost_estimate=pl.CostEstimate(flops=1, bytes_accessed=1, transcendentals=0),
    )(core, mean, *(block for block, _ in raw.values()), *held.values())
    return dict(zip(kept, blocks)), value


def scatter_over_par(message):
    return lax.all_to_all(message, PAR, 0, 0)


def gather_sum(message):
    message = message.reshape(8, 2, *message.shape[1:])
    factor = jnp.exp2(message[:, :, -1:].astype(jnp.float32) - 14.0)
    return jnp.sum(message[:, :, :-1].astype(jnp.float32) * factor, axis=0)


def place_kernel(pieces, place_ref, *refs):
    out_ref = refs[-1]
    for n, (source, index, count) in enumerate(pieces):
        side = round(count**0.5)
        start = place_ref[n] * (side * 128)
        for tile in range(count):
            deep, along = divmod(tile, side)
            column = pl.multiple_of(start + along * 128, 128)
            value = refs[source][(*index[:-1], index[-1] + tile)]
            out_ref[deep * 8 : deep * 8 + 8, pl.ds(column, 128)] = value


def local(block):
    rows = block.shape[0]
    chunk = rows // 16
    blocks = AXES["yh"] * AXES["z"]
    total_rows = rows * blocks
    sy, sz, core = (lax.axis_index(axis).astype(jnp.int32) for axis in ("yh", "z", "core"))
    core = core.reshape(1)

    own = jnp.concatenate([block, permute(block, other_core)], axis=0)
    near = permute(own, along_z)
    mate = permute(own, across_y)

    sums = [jnp.sum(part.astype(jnp.float32), axis=0) for part in (own[:rows], own[rows:])]
    sums = jnp.concatenate(sums).reshape(-1, 128)
    sums = lax.all_to_all(jnp.broadcast_to(sums, (blocks, *sums.shape)), SAMP, 0, 0)
    near, mate, sums = lax.optimization_barrier((near, mate, sums))
    crossed = permute(near, crossing)
    mean = jnp.sum(sums, axis=0).reshape(1, -1) / total_rows
    mean = jnp.broadcast_to(mean, (8, mean.shape[1]))
    scale = float(np.float32(1) / np.sqrt(np.float32(total_rows)))

    raw = {"S0": (own, False), "S1": (near, False), "T1": (mate, False)}
    held, value = multiply(core, mean, raw, {}, ("S0", "S1"), GROUPS[0], scale)
    messages = [scatter_over_par(value.astype(jnp.float16))]
    near, held["S1"] = lax.optimization_barrier((near, held["S1"]))
    far = permute(near, along_z)
    _, value = multiply(core, mean, {"T3": (crossed, True)}, held, (), GROUPS[1], scale)
    messages.append(scatter_over_par(value.astype(jnp.float16)))
    far, crossed, _ = lax.optimization_barrier((far, crossed, value))
    raw = {"S2": (far, False), "T3": (crossed, True)}
    _, value = multiply(core, mean, raw, {"S0": held["S0"]}, (), GROUPS[2], scale)
    messages[1], message = lax.optimization_barrier((messages[1], value.astype(jnp.float16)))
    messages.append(scatter_over_par(message))

    tiles = (rows // 128) ** 2
    sources, pieces, places = [], [], []
    for group, message in zip(GROUPS, messages):
        *sources, message = lax.optimization_barrier((*sources, message))
        done = gather_sum(message)
        sources.append(done)
        leads = {}
        for k, pairs in enumerate(group):
            for c, (left, right) in enumerate(pairs):
                a, b = SLOTS[left][c], SLOTS[right][c]
                offset = (b[0] - a[0]) & 1, (b[1] - a[1]) & 7
                lead = a[0] & 1, a[1] & 7
                if lead == (0, 0):
                    pieces.append((len(sources) - 1, (c, k * tiles), tiles))
                    places.append(offset)
                else:
                    value = done[c, k * tiles : (k + 1) * tiles]
                    leads.setdefault(lead, []).append((offset, value))
        for lead, items in leads.items():
            value = jnp.concatenate([value for _, value in items], axis=0)
            sources.append(permute(value, to_offset(*lead)))
            for n, (offset, _) in enumerate(items):
                pieces.append((len(sources) - 1, (n * tiles,), tiles))
                places.append(offset)
    place = jnp.stack([((sy + dy) & 1) * 8 + ((sz + dz) & 7) for dy, dz in places])
    whole = pl.BlockSpec(memory_space=pltpu.VMEM)
    return pl.pallas_call(
        functools.partial(place_kernel, tuple(pieces)),
        in_specs=[pl.BlockSpec(memory_space=pltpu.SMEM), *(whole for _ in sources)],
        out_specs=whole,
        out_shape=jax.ShapeDtypeStruct((chunk, total_rows), jnp.float32),
        compiler_params=pltpu.CompilerParams(vmem_limit_bytes=8 * 2**20),
    )(place, *sources)


def solution(mesh):
    fine = Mesh(mesh.devices.reshape(tuple(AXES.values())), tuple(AXES))
    return jax.shard_map(
        local,
        mesh=fine,
        in_specs=(P(SAMP, PAR),),
        out_specs=P(SAMP + PAR, None),
        check_vma=False,
    )
```

```python
import functools

import jax
import jax.numpy as jnp
import numpy as np
from jax import lax
from jax.experimental import pallas as pl
from jax.experimental.pallas import tpu as pltpu
from jax.sharding import Mesh, PartitionSpec as P

AXES = {"yh": 2, "z": 8, "x": 4, "yl": 2, "core": 2}
SAMP = ("yh", "z")
PAR = ("x", "yl", "core")
VMEM_MIB = 16
FLOPS = 5 * 10**10

SLOTS = {
    "S0": ((0, 0), (0, 0)),
    "S1": ((0, 1), (0, -1)),
    "S2": ((0, 2), (0, -2)),
    "T1": ((0, 0), (1, 0)),
    "T3": ((0, -2), (1, 2)),
}
GROUPS = (
    ((("S0", "T1"),) * 2, (("S1", "T1"),) * 2, (("T1", "S1"),) * 2),
    ((("T3", "S0"),) * 2, (("S1", "T3"),) * 2, (("T3", "S1"),) * 2),
    ((("S0", "T3"),) * 2, (("T3", "S2"), ("S2", "T3"))),
)


def permute(value, route):
    sizes = tuple(AXES.values())

    def number(place):
        index = 0
        for coordinate, size in zip(place, sizes):
            index = index * size + coordinate % size
        return index

    places = [
        (y, z, x, l, c)
        for y in range(sizes[0])
        for z in range(sizes[1])
        for x in range(sizes[2])
        for l in range(sizes[3])
        for c in range(sizes[4])
    ]
    pairs = [(number(p), number(route(*p))) for p in places if route(*p) is not None]
    return lax.ppermute(value, tuple(AXES), pairs)


def along_z(y, z, x, l, c):
    return (y, z - 1 if c == 0 else z + 1, x, l, c)


def across_y(y, z, x, l, c):
    return (y + 1, z, x, l, 1) if c == 1 else None


def crossing(y, z, x, l, c):
    return (y + 1, z - 1, x, l, 1) if c == 0 else (y, z + 1, x, l, 0)


def other_core(y, z, x, l, c):
    return (y, z, x, l, 1 - c)


def to_offset(dy, dz):
    return lambda y, z, x, l, c: (y + dy, z + dz, x, l, c)


def multiply_kernel(raw, held, kept, group, scale, core_ref, mean_ref, *refs):
    raw_refs, refs = refs[: len(raw)], refs[len(raw) :]
    held_refs, kept_refs, out_ref = refs[: len(held)], refs[len(held) : -1], refs[-1]
    if mean_ref.ndim == 3:
        total = jnp.sum(mean_ref[...], axis=0) * (1.0 / (mean_ref.shape[0] * (raw_refs[0].shape[0] // 2)))
        means = jnp.concatenate([total[n : n + 1] for n in range(total.shape[0])], axis=1)
        kept_refs, (mean_out_ref,) = kept_refs[:-1], kept_refs[-1:]
        mean_out_ref[...] = jnp.broadcast_to(means, mean_out_ref.shape)
    else:
        means = mean_ref[0:1]
    rows, width = raw_refs[0].shape[0] // 2, raw_refs[0].shape[1]
    on_core_1 = core_ref[0] == 1

    terms = [[] for _ in group]
    for half in range(2):
        across = slice(half * width, (half + 1) * width)
        mean = means[:, across]
        wide = {}
        for ref, (name, flip) in zip(raw_refs, raw):
            first = (1 - half if flip else half) * rows
            wide[name] = ref[first : first + rows, :].astype(jnp.float32)
        if "T1" in wide:
            wide["T1"] = jnp.where(on_core_1, wide["T1"], wide["S0"])
        blocks = {
            name: ((value - mean) * scale).astype(jnp.bfloat16) for name, value in wide.items()
        }
        for ref, name in zip(kept_refs, kept):
            ref[:, across] = blocks[name]
        for ref, name in zip(held_refs, held):
            blocks[name] = ref[:, across]
        for term, ((left, right), (left_1, right_1)) in zip(terms, group):
            left, right = blocks[left], blocks[right]
            if left_1 != left:
                left = jnp.where(on_core_1, blocks[left_1], left)
                right = jnp.where(on_core_1, blocks[right_1], right)
            term.append(
                lax.dot_general(
                    left, right, (((1,), (1,)), ((), ())), preferred_element_type=jnp.float32
                )
            )
    totals = [first + second for first, second in terms]
    largest = jnp.zeros((1, 1), jnp.float32)
    for total in totals:
        largest = jnp.maximum(largest, jnp.max(jnp.abs(total), keepdims=True))
    exponent = jnp.clip(jnp.ceil(jnp.log2(largest)), -100.0, 20.0)
    factor = jnp.exp2(14.0 - exponent)
    tile = 0
    for total in totals:
        scaled = (total * factor).reshape(16, rows // 128, 8, rows)
        for deep in range(rows // 128):
            for begin in range(0, rows, 128):
                out_ref[:, tile] = scaled[:, deep, :, begin : begin + 128]
                tile += 1
    out_ref[:, tile] = jnp.broadcast_to(exponent.reshape(1, 1, 1), (16, 8, 128))


def multiply(core, mean, raw, held, kept, group, scale, flops=1):
    first = next(iter(raw.values()))[0]
    rows, width = first.shape[0] // 2, 2 * first.shape[1]
    tiles = len(group) * (rows // 128) ** 2 + 1
    whole = pl.BlockSpec(memory_space=pltpu.VMEM)
    centred = jax.ShapeDtypeStruct((rows, width), jnp.bfloat16)
    names = tuple((name, flip) for name, (_, flip) in raw.items())
    first_round = mean.ndim == 3
    if first_round:
        kept = (*kept, "mean")
    outs = [jax.ShapeDtypeStruct((8, width), jnp.float32) if n == "mean" else centred for n in kept]
    *blocks, value = pl.pallas_call(
        functools.partial(multiply_kernel, names, tuple(held), kept[: len(kept) - first_round], group, scale),
        in_specs=[pl.BlockSpec(memory_space=pltpu.SMEM)] + [whole] * (1 + len(raw) + len(held)),
        out_specs=[whole] * (len(kept) + 1),
        out_shape=[*outs, jax.ShapeDtypeStruct((16, tiles, 8, 128), jnp.float32)],
        compiler_params=pltpu.CompilerParams(vmem_limit_bytes=VMEM_MIB * 2**20),
        cost_estimate=pl.CostEstimate(flops=flops, bytes_accessed=1, transcendentals=0),
    )(core, mean, *(block for block, _ in raw.values()), *held.values())
    return dict(zip(kept, blocks)), value


def scatter_over_par(message):
    return lax.all_to_all(message, PAR, 0, 0)


def gather_sum(message):
    message = message.reshape(8, 2, *message.shape[1:])
    factor = jnp.exp2(message[:, :, -1:].astype(jnp.float32) - 14.0)
    return jnp.sum(message[:, :, :-1].astype(jnp.float32) * factor, axis=0)


def place_kernel(pieces, place_ref, *refs):
    out_ref = refs[-1]
    for n, (source, index, count) in enumerate(pieces):
        side = round(count**0.5)
        start = place_ref[n] * (side * 128)
        for tile in range(count):
            deep, along = divmod(tile, side)
            column = pl.multiple_of(start + along * 128, 128)
            value = refs[source][(*index[:-1], index[-1] + tile)]
            out_ref[deep * 8 : deep * 8 + 8, pl.ds(column, 128)] = value


def local(block):
    rows = block.shape[0]
    chunk = rows // 16
    blocks = AXES["yh"] * AXES["z"]
    total_rows = rows * blocks
    sy, sz, core = (lax.axis_index(axis).astype(jnp.int32) for axis in ("yh", "z", "core"))
    core = core.reshape(1)

    own = jnp.concatenate([block, permute(block, other_core)], axis=0)
    near = permute(own, along_z)
    mate = permute(own, across_y)

    sums = [jnp.sum(part.astype(jnp.float32), axis=0) for part in (own[:rows], own[rows:])]
    sums = jnp.concatenate(sums).reshape(-1, 128)
    sums = lax.all_to_all(jnp.broadcast_to(sums, (blocks, *sums.shape)), SAMP, 0, 0)
    crossed = permute(near, crossing)
    scale = float(np.float32(1) / np.sqrt(np.float32(total_rows)))

    raw = {"S0": (own, False), "S1": (near, False), "T1": (mate, False)}
    held, value = multiply(core, sums, raw, {}, ("S0", "S1"), GROUPS[0], scale, FLOPS)
    mean = held.pop("mean")
    messages = [scatter_over_par(value.astype(jnp.float16))]
    near, held["S1"] = lax.optimization_barrier((near, held["S1"]))
    far = permute(near, along_z)
    _, value = multiply(core, mean, {"T3": (crossed, True)}, held, (), GROUPS[1], scale)
    messages.append(scatter_over_par(value.astype(jnp.float16)))
    far, crossed, _ = lax.optimization_barrier((far, crossed, value))
    raw = {"S2": (far, False), "T3": (crossed, True)}
    _, value = multiply(core, mean, raw, {"S0": held["S0"]}, (), GROUPS[2], scale)
    messages[1], message = lax.optimization_barrier((messages[1], value.astype(jnp.float16)))
    messages.append(scatter_over_par(message))

    tiles = (rows // 128) ** 2
    sources, pieces, places = [], [], []
    for group, message in zip(GROUPS, messages):
        *sources, message = lax.optimization_barrier((*sources, message))
        done = gather_sum(message)
        sources.append(done)
        leads = {}
        for k, pairs in enumerate(group):
            for c, (left, right) in enumerate(pairs):
                a, b = SLOTS[left][c], SLOTS[right][c]
                offset = (b[0] - a[0]) & 1, (b[1] - a[1]) & 7
                lead = a[0] & 1, a[1] & 7
                if lead == (0, 0):
                    pieces.append((len(sources) - 1, (c, k * tiles), tiles))
                    places.append(offset)
                else:
                    value = done[c, k * tiles : (k + 1) * tiles]
                    leads.setdefault(lead, []).append((offset, value))
        for lead, items in leads.items():
            value = jnp.concatenate([value for _, value in items], axis=0)
            sources.append(permute(value, to_offset(*lead)))
            for n, (offset, _) in enumerate(items):
                pieces.append((len(sources) - 1, (n * tiles,), tiles))
                places.append(offset)
    place = jnp.stack([((sy + dy) & 1) * 8 + ((sz + dz) & 7) for dy, dz in places])
    whole = pl.BlockSpec(memory_space=pltpu.VMEM)
    return pl.pallas_call(
        functools.partial(place_kernel, tuple(pieces)),
        in_specs=[pl.BlockSpec(memory_space=pltpu.SMEM), *(whole for _ in sources)],
        out_specs=whole,
        out_shape=jax.ShapeDtypeStruct((chunk, total_rows), jnp.float32),
        compiler_params=pltpu.CompilerParams(vmem_limit_bytes=8 * 2**20),
    )(place, *sources)


def solution(mesh):
    fine = Mesh(mesh.devices.reshape(tuple(AXES.values())), tuple(AXES))
    return jax.shard_map(
        local,
        mesh=fine,
        in_specs=(P(SAMP, PAR),),
        out_specs=P(SAMP + PAR, None),
        check_vma=False,
    )
```

```python
import functools

import jax
import jax.numpy as jnp
import numpy as np
from jax import lax
from jax.experimental import pallas as pl
from jax.experimental.pallas import tpu as pltpu
from jax.sharding import Mesh, PartitionSpec as P

AXES = {"yh": 2, "z": 8, "x": 4, "yl": 2, "core": 2}
SAMP = ("yh", "z")
PAR = ("x", "yl", "core")
VMEM_MIB = 16
FLOPS = 5 * 10**10

SLOTS = {
    "S0": ((0, 0), (0, 0)),
    "S1": ((0, 1), (0, -1)),
    "S2": ((0, 2), (0, -2)),
    "T1": ((0, 0), (1, 0)),
    "T3": ((0, -2), (1, 2)),
}
GROUPS = (
    ((("S0", "T1"),) * 2, (("S1", "T1"),) * 2, (("T1", "S1"),) * 2),
    ((("T3", "S0"),) * 2, (("S1", "T3"),) * 2, (("T3", "S1"),) * 2),
    ((("S0", "T3"),) * 2, (("T3", "S2"), ("S2", "T3"))),
)


def permute(value, route):
    sizes = tuple(AXES.values())

    def number(place):
        index = 0
        for coordinate, size in zip(place, sizes):
            index = index * size + coordinate % size
        return index

    places = [
        (y, z, x, l, c)
        for y in range(sizes[0])
        for z in range(sizes[1])
        for x in range(sizes[2])
        for l in range(sizes[3])
        for c in range(sizes[4])
    ]
    pairs = [(number(p), number(route(*p))) for p in places if route(*p) is not None]
    return lax.ppermute(value, tuple(AXES), pairs)


def along_z(y, z, x, l, c):
    return (y, z - 1 if c == 0 else z + 1, x, l, c)


def across_y(y, z, x, l, c):
    return (y + 1, z, x, l, 1) if c == 1 else None


def crossing(y, z, x, l, c):
    return (y + 1, z - 1, x, l, 1) if c == 0 else (y, z + 1, x, l, 0)


def other_core(y, z, x, l, c):
    return (y, z, x, l, 1 - c)


def to_offset(dy, dz):
    return lambda y, z, x, l, c: (y + dy, z + dz, x, l, c)


def multiply_kernel(raw, held, kept, group, scale, core_ref, mean_ref, *refs):
    raw_refs, refs = refs[: len(raw)], refs[len(raw) :]
    held_refs, kept_refs, out_ref = refs[: len(held)], refs[len(held) : -1], refs[-1]
    if mean_ref.ndim == 3:
        total = jnp.sum(mean_ref[...], axis=0) * (1.0 / (mean_ref.shape[0] * (raw_refs[0].shape[0] // 2)))
        means = jnp.concatenate([total[n : n + 1] for n in range(total.shape[0])], axis=1)
        kept_refs, (mean_out_ref,) = kept_refs[:-1], kept_refs[-1:]
        mean_out_ref[...] = jnp.broadcast_to(means, mean_out_ref.shape)
    else:
        means = mean_ref[0:1]
    rows, width = raw_refs[0].shape[0] // 2, raw_refs[0].shape[1]
    on_core_1 = core_ref[0] == 1

    terms = [[] for _ in group]
    for half in range(2):
        across = slice(half * width, (half + 1) * width)
        mean = means[:, across]
        wide = {}
        for ref, (name, flip) in zip(raw_refs, raw):
            first = (1 - half if flip else half) * rows
            wide[name] = ref[first : first + rows, :].astype(jnp.float32)
        if "T1" in wide:
            wide["T1"] = jnp.where(on_core_1, wide["T1"], wide["S0"])
        blocks = {
            name: ((value - mean) * scale).astype(jnp.bfloat16) for name, value in wide.items()
        }
        for ref, name in zip(kept_refs, kept):
            ref[:, across] = blocks[name]
        for ref, name in zip(held_refs, held):
            blocks[name] = ref[:, across]
        for term, ((left, right), (left_1, right_1)) in zip(terms, group):
            same = (left, right) == (left_1, right_1)
            left, right = blocks[left], blocks[right]
            if not same:
                left = jnp.where(on_core_1, blocks[left_1], left)
                right = jnp.where(on_core_1, blocks[right_1], right)
            term.append(
                lax.dot_general(
                    left, right, (((1,), (1,)), ((), ())), preferred_element_type=jnp.float32
                )
            )
    totals = [first + second for first, second in terms]
    largest = jnp.zeros((1, 1), jnp.float32)
    for total in totals:
        largest = jnp.maximum(largest, jnp.max(jnp.abs(total), keepdims=True))
    exponent = jnp.clip(jnp.ceil(jnp.log2(largest)), -100.0, 20.0)
    factor = jnp.exp2(14.0 - exponent)
    tile = 0
    for total in totals:
        scaled = (total * factor).reshape(16, rows // 128, 8, rows)
        for deep in range(rows // 128):
            for begin in range(0, rows, 128):
                out_ref[:, tile] = scaled[:, deep, :, begin : begin + 128]
                tile += 1
    out_ref[:, tile] = jnp.broadcast_to(exponent.reshape(1, 1, 1), (16, 8, 128))


def multiply(core, mean, raw, held, kept, group, scale, flops=1):
    first = next(iter(raw.values()))[0]
    rows, width = first.shape[0] // 2, 2 * first.shape[1]
    tiles = len(group) * (rows // 128) ** 2 + 1
    whole = pl.BlockSpec(memory_space=pltpu.VMEM)
    centred = jax.ShapeDtypeStruct((rows, width), jnp.bfloat16)
    names = tuple((name, flip) for name, (_, flip) in raw.items())
    first_round = mean.ndim == 3
    if first_round:
        kept = (*kept, "mean")
    outs = [jax.ShapeDtypeStruct((8, width), jnp.float32) if n == "mean" else centred for n in kept]
    *blocks, value = pl.pallas_call(
        functools.partial(multiply_kernel, names, tuple(held), kept[: len(kept) - first_round], group, scale),
        in_specs=[pl.BlockSpec(memory_space=pltpu.SMEM)] + [whole] * (1 + len(raw) + len(held)),
        out_specs=[whole] * (len(kept) + 1),
        out_shape=[*outs, jax.ShapeDtypeStruct((16, tiles, 8, 128), jnp.float32)],
        compiler_params=pltpu.CompilerParams(vmem_limit_bytes=VMEM_MIB * 2**20),
        cost_estimate=pl.CostEstimate(flops=flops, bytes_accessed=1, transcendentals=0),
    )(core, mean, *(block for block, _ in raw.values()), *held.values())
    return dict(zip(kept, blocks)), value


def scatter_over_par(message):
    return lax.all_to_all(message, PAR, 0, 0)


def gather_sum(message):
    message = message.reshape(8, 2, *message.shape[1:])
    factor = jnp.exp2(message[:, :, -1:].astype(jnp.float32) - 14.0)
    return jnp.sum(message[:, :, :-1].astype(jnp.float32) * factor, axis=0)


def place_kernel(pieces, place_ref, *refs):
    out_ref = refs[-1]
    for n, (source, index, count) in enumerate(pieces):
        side = round(count**0.5)
        start = place_ref[n] * (side * 128)
        for tile in range(count):
            deep, along = divmod(tile, side)
            column = pl.multiple_of(start + along * 128, 128)
            value = refs[source][(*index[:-1], index[-1] + tile)]
            out_ref[deep * 8 : deep * 8 + 8, pl.ds(column, 128)] = value


def local(block):
    rows = block.shape[0]
    chunk = rows // 16
    blocks = AXES["yh"] * AXES["z"]
    total_rows = rows * blocks
    sy, sz, core = (lax.axis_index(axis).astype(jnp.int32) for axis in ("yh", "z", "core"))
    core = core.reshape(1)

    own = jnp.concatenate([block, permute(block, other_core)], axis=0)
    near = permute(own, along_z)
    mate = permute(own, across_y)

    sums = [jnp.sum(part.astype(jnp.float32), axis=0) for part in (own[:rows], own[rows:])]
    sums = jnp.concatenate(sums).reshape(-1, 128)
    sums = lax.all_to_all(jnp.broadcast_to(sums, (blocks, *sums.shape)), SAMP, 0, 0)
    crossed = permute(near, crossing)
    scale = float(np.float32(1) / np.sqrt(np.float32(total_rows)))

    raw = {"S0": (own, False), "S1": (near, False), "T1": (mate, False)}
    held, value = multiply(core, sums, raw, {}, ("S0", "S1"), GROUPS[0], scale, FLOPS)
    mean = held.pop("mean")
    messages = [scatter_over_par(value.astype(jnp.float16))]
    near, held["S1"] = lax.optimization_barrier((near, held["S1"]))
    far = permute(near, along_z)
    _, value = multiply(core, mean, {"T3": (crossed, True)}, held, (), GROUPS[1], scale)
    messages.append(scatter_over_par(value.astype(jnp.float16)))
    far, crossed, _ = lax.optimization_barrier((far, crossed, value))
    raw = {"S2": (far, False), "T3": (crossed, True)}
    _, value = multiply(core, mean, raw, {"S0": held["S0"]}, (), GROUPS[2], scale)
    messages[1], message = lax.optimization_barrier((messages[1], value.astype(jnp.float16)))
    messages.append(scatter_over_par(message))

    tiles = (rows // 128) ** 2
    sources, pieces, places = [], [], []
    for group, message in zip(GROUPS, messages):
        *sources, message = lax.optimization_barrier((*sources, message))
        done = gather_sum(message)
        sources.append(done)
        leads = {}
        for k, pairs in enumerate(group):
            for c, (left, right) in enumerate(pairs):
                a, b = SLOTS[left][c], SLOTS[right][c]
                offset = (b[0] - a[0]) & 1, (b[1] - a[1]) & 7
                lead = a[0] & 1, a[1] & 7
                if lead == (0, 0):
                    pieces.append((len(sources) - 1, (c, k * tiles), tiles))
                    places.append(offset)
                else:
                    value = done[c, k * tiles : (k + 1) * tiles]
                    leads.setdefault(lead, []).append((offset, value))
        for lead, items in leads.items():
            value = jnp.concatenate([value for _, value in items], axis=0)
            sources.append(permute(value, to_offset(*lead)))
            for n, (offset, _) in enumerate(items):
                pieces.append((len(sources) - 1, (n * tiles,), tiles))
                places.append(offset)
    place = jnp.stack([((sy + dy) & 1) * 8 + ((sz + dz) & 7) for dy, dz in places])
    whole = pl.BlockSpec(memory_space=pltpu.VMEM)
    return pl.pallas_call(
        functools.partial(place_kernel, tuple(pieces)),
        in_specs=[pl.BlockSpec(memory_space=pltpu.SMEM), *(whole for _ in sources)],
        out_specs=whole,
        out_shape=jax.ShapeDtypeStruct((chunk, total_rows), jnp.float32),
        compiler_params=pltpu.CompilerParams(vmem_limit_bytes=8 * 2**20),
    )(place, *sources)


def solution(mesh):
    fine = Mesh(mesh.devices.reshape(tuple(AXES.values())), tuple(AXES))
    return jax.shard_map(
        local,
        mesh=fine,
        in_specs=(P(SAMP, PAR),),
        out_specs=P(SAMP + PAR, None),
        check_vma=False,
    )
```

```python
import functools

import jax
import jax.numpy as jnp
import numpy as np
from jax import lax
from jax.experimental import pallas as pl
from jax.experimental.pallas import tpu as pltpu
from jax.sharding import Mesh, PartitionSpec as P

AXES = {"yh": 2, "z": 8, "x": 4, "yl": 2, "core": 2}
SAMP = ("yh", "z")
PAR = ("x", "yl", "core")
VMEM_MIB = 16
FLOPS = 5 * 10**10

SLOTS = {
    "S0": ((0, 0), (0, 0)),
    "S1": ((0, 1), (0, -1)),
    "S2": ((0, 2), (0, -2)),
    "T1": ((0, 0), (1, 0)),
    "T3": ((0, -2), (1, 2)),
}
GROUPS = (
    ((("S0", "T1"),) * 2, (("S1", "T1"),) * 2, (("T1", "S1"),) * 2),
    ((("T3", "S0"),) * 2, (("S1", "T3"),) * 2, (("T3", "S1"),) * 2),
    ((("S0", "T3"),) * 2, (("T3", "S2"), ("S2", "T3"))),
)


def permute(value, route):
    sizes = tuple(AXES.values())

    def number(place):
        index = 0
        for coordinate, size in zip(place, sizes):
            index = index * size + coordinate % size
        return index

    places = [
        (y, z, x, l, c)
        for y in range(sizes[0])
        for z in range(sizes[1])
        for x in range(sizes[2])
        for l in range(sizes[3])
        for c in range(sizes[4])
    ]
    pairs = [(number(p), number(route(*p))) for p in places if route(*p) is not None]
    return lax.ppermute(value, tuple(AXES), pairs)


def along_z(y, z, x, l, c):
    return (y, z - 1 if c == 0 else z + 1, x, l, c)


def across_y(y, z, x, l, c):
    return (y + 1, z, x, l, 1) if c == 1 else None


def crossing(y, z, x, l, c):
    return (y + 1, z - 1, x, l, 1) if c == 0 else (y, z + 1, x, l, 0)


def other_core(y, z, x, l, c):
    return (y, z, x, l, 1 - c)


def to_offset(dy, dz):
    return lambda y, z, x, l, c: (y + dy, z + dz, x, l, c)


def multiply_kernel(raw, held, kept, group, scale, core_ref, mean_ref, *refs):
    raw_refs, refs = refs[: len(raw)], refs[len(raw) :]
    held_refs, kept_refs, out_ref = refs[: len(held)], refs[len(held) : -1], refs[-1]
    if mean_ref.ndim == 3:
        total = jnp.sum(mean_ref[...], axis=0) * (1.0 / (mean_ref.shape[0] * (raw_refs[0].shape[0] // 2)))
        means = jnp.concatenate([total[n : n + 1] for n in range(total.shape[0])], axis=1)
        kept_refs, (mean_out_ref,) = kept_refs[:-1], kept_refs[-1:]
        mean_out_ref[...] = jnp.broadcast_to(means, mean_out_ref.shape)
    else:
        means = mean_ref[0:1]
    rows, width = raw_refs[0].shape[0] // 2, raw_refs[0].shape[1]
    on_core_1 = core_ref[0] == 1

    terms = [[] for _ in group]
    for half in range(2):
        across = slice(half * width, (half + 1) * width)
        mean = means[:, across]
        wide = {}
        for ref, (name, flip) in zip(raw_refs, raw):
            first = (1 - half if flip else half) * rows
            wide[name] = ref[first : first + rows, :].astype(jnp.float32)
        if "T1" in wide:
            wide["T1"] = jnp.where(on_core_1, wide["T1"], wide["S0"])
        blocks = {
            name: ((value - mean) * scale).astype(jnp.bfloat16) for name, value in wide.items()
        }
        for ref, name in zip(kept_refs, kept):
            ref[:, across] = blocks[name]
        for ref, name in zip(held_refs, held):
            blocks[name] = ref[:, across]
        for term, ((left, right), (left_1, right_1)) in zip(terms, group):
            same = (left, right) == (left_1, right_1)
            left, right = blocks[left], blocks[right]
            if not same:
                left = jnp.where(on_core_1, blocks[left_1], left)
                right = jnp.where(on_core_1, blocks[right_1], right)
            term.append(
                lax.dot_general(
                    left, right, (((1,), (1,)), ((), ())), preferred_element_type=jnp.float32
                )
            )
    totals = [first + second for first, second in terms]
    largest = jnp.zeros((1, 1), jnp.float32)
    for total in totals:
        largest = jnp.maximum(largest, jnp.max(jnp.abs(total), keepdims=True))
    exponent = jnp.clip(jnp.ceil(jnp.log2(largest)), -100.0, 20.0)
    factor = jnp.exp2(14.0 - exponent)
    tile = 0
    for total in totals:
        scaled = (total * factor).reshape(16, rows // 128, 8, rows)
        for deep in range(rows // 128):
            for begin in range(0, rows, 128):
                out_ref[:, tile] = scaled[:, deep, :, begin : begin + 128]
                tile += 1
    out_ref[:, tile] = jnp.broadcast_to(exponent.reshape(1, 1, 1), (16, 8, 128))


def multiply(core, mean, raw, held, kept, group, scale, flops=1):
    first = next(iter(raw.values()))[0]
    rows, width = first.shape[0] // 2, 2 * first.shape[1]
    tiles = len(group) * (rows // 128) ** 2 + 1
    whole = pl.BlockSpec(memory_space=pltpu.VMEM)
    centred = jax.ShapeDtypeStruct((rows, width), jnp.bfloat16)
    names = tuple((name, flip) for name, (_, flip) in raw.items())
    first_round = mean.ndim == 3
    if first_round:
        kept = (*kept, "mean")
    outs = [jax.ShapeDtypeStruct((8, width), jnp.float32) if n == "mean" else centred for n in kept]
    *blocks, value = pl.pallas_call(
        functools.partial(multiply_kernel, names, tuple(held), kept[: len(kept) - first_round], group, scale),
        in_specs=[pl.BlockSpec(memory_space=pltpu.SMEM)] + [whole] * (1 + len(raw) + len(held)),
        out_specs=[whole] * (len(kept) + 1),
        out_shape=[*outs, jax.ShapeDtypeStruct((16, tiles, 8, 128), jnp.float32)],
        compiler_params=pltpu.CompilerParams(vmem_limit_bytes=VMEM_MIB * 2**20),
        cost_estimate=pl.CostEstimate(flops=flops, bytes_accessed=1, transcendentals=0),
    )(core, mean, *(block for block, _ in raw.values()), *held.values())
    return dict(zip(kept, blocks)), value


def scatter_over_par(message):
    return lax.all_to_all(message, PAR, 0, 0)


def gather_sum(message):
    message = message.reshape(8, 2, *message.shape[1:])
    factor = jnp.exp2(message[:, :, -1:].astype(jnp.float32) - 14.0)
    return jnp.sum(message[:, :, :-1].astype(jnp.float32) * factor, axis=0)


def place_kernel(pieces, place_ref, *refs):
    out_ref = refs[-1]
    for n, (source, index, count) in enumerate(pieces):
        side = round(count**0.5)
        start = place_ref[n] * (side * 128)
        for tile in range(count):
            deep, along = divmod(tile, side)
            column = pl.multiple_of(start + along * 128, 128)
            value = refs[source][(*index[:-1], index[-1] + tile)]
            out_ref[deep * 8 : deep * 8 + 8, pl.ds(column, 128)] = value


def local(block):
    rows = block.shape[0]
    chunk = rows // 16
    blocks = AXES["yh"] * AXES["z"]
    total_rows = rows * blocks
    sy, sz, core = (lax.axis_index(axis).astype(jnp.int32) for axis in ("yh", "z", "core"))
    core = core.reshape(1)

    own = jnp.concatenate([block, permute(block, other_core)], axis=0)
    near = permute(own, along_z)
    mate = permute(own, across_y)

    sums = [jnp.sum(part.astype(jnp.float32), axis=0) for part in (own[:rows], own[rows:])]
    sums = jnp.concatenate(sums).reshape(-1, 128)
    sums = lax.all_to_all(jnp.broadcast_to(sums, (blocks, *sums.shape)), SAMP, 0, 0)
    crossed = permute(near, crossing)
    scale = float(np.float32(1) / np.sqrt(np.float32(total_rows)))

    raw = {"S0": (own, False), "S1": (near, False), "T1": (mate, False)}
    held, value = multiply(core, sums, raw, {}, (), GROUPS[0], scale, FLOPS)
    mean = held.pop("mean")
    messages = [scatter_over_par(value.astype(jnp.float16))]
    near, mean = lax.optimization_barrier((near, mean))
    far = permute(near, along_z)
    raw = {"S0": (own, False), "S1": (near, False), "T3": (crossed, True)}
    _, value = multiply(core, mean, raw, {}, (), GROUPS[1], scale)
    messages.append(scatter_over_par(value.astype(jnp.float16)))
    far, crossed, _ = lax.optimization_barrier((far, crossed, value))
    raw = {"S0": (own, False), "S2": (far, False), "T3": (crossed, True)}
    _, value = multiply(core, mean, raw, {}, (), GROUPS[2], scale)
    messages[1], message = lax.optimization_barrier((messages[1], value.astype(jnp.float16)))
    messages.append(scatter_over_par(message))

    tiles = (rows // 128) ** 2
    sources, pieces, places = [], [], []
    for group, message in zip(GROUPS, messages):
        *sources, message = lax.optimization_barrier((*sources, message))
        done = gather_sum(message)
        sources.append(done)
        leads = {}
        for k, pairs in enumerate(group):
            for c, (left, right) in enumerate(pairs):
                a, b = SLOTS[left][c], SLOTS[right][c]
                offset = (b[0] - a[0]) & 1, (b[1] - a[1]) & 7
                lead = a[0] & 1, a[1] & 7
                if lead == (0, 0):
                    pieces.append((len(sources) - 1, (c, k * tiles), tiles))
                    places.append(offset)
                else:
                    value = done[c, k * tiles : (k + 1) * tiles]
                    leads.setdefault(lead, []).append((offset, value))
        for lead, items in leads.items():
            value = jnp.concatenate([value for _, value in items], axis=0)
            sources.append(permute(value, to_offset(*lead)))
            for n, (offset, _) in enumerate(items):
                pieces.append((len(sources) - 1, (n * tiles,), tiles))
                places.append(offset)
    place = jnp.stack([((sy + dy) & 1) * 8 + ((sz + dz) & 7) for dy, dz in places])
    whole = pl.BlockSpec(memory_space=pltpu.VMEM)
    return pl.pallas_call(
        functools.partial(place_kernel, tuple(pieces)),
        in_specs=[pl.BlockSpec(memory_space=pltpu.SMEM), *(whole for _ in sources)],
        out_specs=whole,
        out_shape=jax.ShapeDtypeStruct((chunk, total_rows), jnp.float32),
        compiler_params=pltpu.CompilerParams(vmem_limit_bytes=8 * 2**20),
    )(place, *sources)


def solution(mesh):
    fine = Mesh(mesh.devices.reshape(tuple(AXES.values())), tuple(AXES))
    return jax.shard_map(
        local,
        mesh=fine,
        in_specs=(P(SAMP, PAR),),
        out_specs=P(SAMP + PAR, None),
        check_vma=False,
    )
```
